256 devices in a mesh: shard: 64 (over z, y, core), dim: 4 (over x).
Axes of the slice: x: 4, y: 4, z: 8, core: 2. Of those that a mesh axis runs over, the one named last changes fastest.
Arguments:
- queries: bfloat16 [128, 16384], P('dim', 'shard'), may hold values from -0.69921875 to 0.69921875
- passages: bfloat16 [128, 524288], P('dim', 'shard'), may hold values from -0.69921875 to 0.69921875
- cand_ids: int32 [512, 2048], P('dim', 'shard'), may hold values from 0 to 127
- counts: int32 [512, 64], P('dim', 'shard'), may hold values from 16 to 32, as said below
Outputs:
- cand_scores: float32 [512, 2048], P('dim', 'shard')
- top_scores: float32 [512, 100], P('dim')
The draws below stay inside these ranges and needn't reach their ends.
Inputs may be any that keep to these rules, and one draw needn't show every extreme that they name: `counts`: every shard's block of every query has between 16 and 32 live slots, and query 0 has all 32 live on every shard.
All inputs are finite; a program needn't handle non-finite values.
Results may differ from the reference program's by a relative error of at most 0.0003.
Values may be sent and summed in bfloat16 or wider, within the bound.
No kernel may reach another device: no remote copies, remote signals or barrier semaphores. Data moves between devices by JAX's collectives and lax.ppermute only.
A program may use at most 64 MiB of HBM per device.

```python
import jax
import jax.numpy as jnp
from jax import lax

EMB = 128
QTOK = 32
DOC_TOK = 64
TOPK = 100
CAND = 32
PASS_DEV = 128
QUERIES = 512
PASSAGES = 8192
N_SHARD = 64


def draw_counts(key, part):
    key = jax.random.fold_in(key, 5)
    first_key, second_key = jax.random.split(key)
    lowest = CAND // 2
    ceiling = jax.random.randint(first_key, (1, N_SHARD), lowest, CAND + 1)
    drawn = jax.random.randint(second_key, (QUERIES, N_SHARD), lowest, ceiling + 1)
    drawn = drawn.at[0, :].set(CAND)
    return drawn.astype(jnp.int32)


def set_ends(result, rng, least, high):
    longest = result.shape.index(max(result.shape))
    spots = []
    for shift in (0, 1):
        where = [jax.random.randint(jax.random.fold_in(rng, axis), (), 0, length) for axis, length in enumerate(result.shape)]
        where[longest] = (where[longest] + shift) % result.shape[longest]
        spots.append(tuple(where))
    return result.at[spots[0]].set(least).at[spots[1]].set(high)


def shard_levels(key, shape, cuts, least, top_value):
    def one(position, blocks):
        heights = jax.random.uniform(jax.random.fold_in(jax.random.fold_in(key, 6), position), (blocks,), jnp.float32, least / len(cuts), top_value / len(cuts))
        return jnp.repeat(jnp.exp(heights), shape[position] // blocks).reshape((-1,) + (1,) * (len(shape) - position - 1))

    factor_of = one(*cuts[0])
    for cut in cuts[1:]:
        factor_of = factor_of * one(*cut)
    return factor_of


def gaussian(stream_key, shape, scale, most, shards=(), held_as=jnp.bfloat16):
    level = shard_levels(stream_key, shape, shards, -0.22, 0.18) if shards else 1.0
    values = jax.random.normal(stream_key, shape, jnp.float32) * scale * level
    return jnp.minimum(jnp.maximum(values, -most), most).astype(held_as)


def setup_inputs(seed: int = 0) -> dict:
    keys = jax.random.split(jax.random.key(seed), 5)
    queries = gaussian(keys[0], (EMB, QUERIES * QTOK), 0.0884, 0.69921875, ((0, 4), (1, 64)))
    passages = gaussian(keys[1], (EMB, PASSAGES * DOC_TOK), 0.0884, 0.69921875, ((0, 4), (1, 64)))
    cand_ids = set_ends(jax.random.randint(keys[2], (QUERIES, N_SHARD * CAND), 0, PASS_DEV), jax.random.fold_in(keys[2], 1), 0, PASS_DEV - 1).astype(jnp.int32)
    counts = draw_counts(jax.random.fold_in(keys[4], 71), 0)
    return {"queries": queries, "passages": passages, "cand_ids": cand_ids, "counts": counts}


def reference(queries, passages, cand_ids, counts):
    query_tok = jnp.transpose(queries).reshape(QUERIES, QTOK, EMB)
    doc_tok = jnp.transpose(passages).reshape(PASSAGES, DOC_TOK, EMB)
    columns = jnp.arange(N_SHARD * CAND, dtype=jnp.int32)
    offsets = (columns // CAND) * PASS_DEV
    slot_index = columns % CAND

    def one_query(items):
        query_vec, id_row, count_row = items
        picked = doc_tok[(id_row + offsets).astype(jnp.int32)].astype(jnp.float32)
        tokens = jnp.einsum("te,cle->ctl", query_vec.astype(jnp.float32), picked)
        score = jnp.mean(jnp.max(tokens, axis=2), axis=1)
        live = slot_index < jnp.repeat(count_row, CAND)
        kept = jnp.where(live, score, jnp.float32(0.0))
        best = lax.top_k(jnp.where(live, score, jnp.float32(-1e30)), TOPK)[0]
        return kept, best

    cand_scores, top_scores = lax.map(one_query, (query_tok, cand_ids, counts))
    return cand_scores, top_scores
```

```python
import jax
import jax.numpy as jnp
from jax import lax
from jax.experimental import pallas as pl
from jax.experimental.pallas import tpu as pltpu
from jax.sharding import Mesh, PartitionSpec as P

DOC_TOK = 64
QTOK = 32
TOPK = 100
LOWEST = -1e30
SHARD = ("zh", "zl", "y", "core")
ALL = SHARD + ("dim",)


def transpose_docs(d0, d1, d2, d3, out):
    rows = d0.shape[0]
    step = 512
    for start in range(0, d0.shape[1], step):
        cols = slice(start, start + step)
        block = jnp.concatenate([d[:, cols] for d in (d0, d1, d2, d3)], axis=0)
        out[cols, :] = jnp.transpose(block)


def docs_kernel(d0, d1, d2, d3, out):
    transpose_docs(d0, d1, d2, d3, out)


def score_kernel(docs, qa, qb, ids, counts, cand, send, best, kept):
    core = lax.axis_index("core")
    turn = lax.rem(lax.axis_index("zh") - lax.axis_index("dim") + 4, 4)
    docs_n = best.shape[0]
    sources = qa.shape[0]
    slots = ids.shape[1]
    tile = 512
    per = tile // DOC_TOK

    def one(source, q, side):
        weights = jnp.concatenate([q[source, lax.rem(turn + k, 4)] for k in range(4)], axis=0)
        for t in range(docs_n // per):
            tokens = jnp.dot(docs[t * tile : (t + 1) * tile, :], weights, preferred_element_type=jnp.float32)
            best[t * per : (t + 1) * per, :] = jnp.max(tokens.reshape(per, DOC_TOK, tokens.shape[1]), axis=1)
        turned = jnp.transpose(best[...])
        mean = jnp.sum(turned.reshape(-1, QTOK, docs_n), axis=1) * (1.0 / QTOK)
        queries = mean.shape[0]
        rows = pl.ds(pl.multiple_of((source * 2 + side) * queries, queries), queries)
        index = jnp.concatenate([ids[rows, :], jnp.zeros((queries, docs_n - slots), jnp.int32)], axis=1)
        kept[rows, :] = jnp.take_along_axis(mean, index, axis=1)

    def pair(source, carry):
        one(source, qa, core)
        one(source, qb, 1 - core)
        return carry

    lax.fori_loop(0, sources, pair, 0)
    scores = kept[...]
    live = lax.broadcasted_iota(jnp.int32, scores.shape, 1) < counts[...]
    cand[...] = jnp.where(live, scores, 0.0)[:, :slots]
    masked = jnp.transpose(jnp.where(live, scores, LOWEST))[:slots, :]
    half = masked.shape[1] // 2
    send[...] = jnp.where(core == 0, masked, pltpu.roll(masked, half, 1))


def exchange(values, i, j):
    a, b = values[i], values[j]
    values[i] = jnp.maximum(a, b)
    values[j] = jnp.minimum(a, b)


def odd_even_merge(values, lo, n, r):
    m = r * 2
    if m < n:
        odd_even_merge(values, lo, n, m)
        odd_even_merge(values, lo + r, n, m)
        for i in range(lo + r, lo + n - r, m):
            exchange(values, i, i + r)
    else:
        exchange(values, lo, lo + r)


def odd_even_sort(values, lo, n):
    if n > 1:
        m = n // 2
        odd_even_sort(values, lo, m)
        odd_even_sort(values, lo + m, m)
        odd_even_merge(values, lo, n, 1)


def clean(values, lo, n):
    if n > 1:
        m = n // 2
        for i in range(m):
            exchange(values, lo + i, lo + i + m)
        clean(values, lo, m)
        clean(values, lo + m, m)


def top_kernel(pieces, out):
    count = pieces.shape[0]
    values = [pieces[i] for i in range(count)]
    odd_even_sort(values, 0, count)
    for axis, shift in ((1, 64), (0, 4), (0, 2), (0, 1)):
        other = [pltpu.roll(v, shift, axis) for v in values]
        values = [jnp.maximum(values[i], other[count - 1 - i]) for i in range(count)]
        clean(values, 0, count)
    stacked = jnp.concatenate([v[0:1, :] for v in values], axis=0)
    out[...] = jnp.transpose(stacked)


def vmem(n):
    return [pl.BlockSpec(memory_space=pltpu.VMEM)] * n


def shards(queries, passages, cand_ids, counts):
    sizes = {a: lax.axis_size(a) for a in ALL}
    flat = lambda zh, zl, y, c, x: (((zh * 2 + zl) * 4 + y) * 2 + c) * 4 + x
    moves = [
        [
            (flat(zh, zl, y, c, x), flat((x + j) % 4, zl, y, c, zh))
            for zh in range(4)
            for zl in range(2)
            for y in range(4)
            for c in range(2)
            for x in range(4)
        ]
        for j in range(4)
    ]
    parts = jnp.stack([lax.ppermute(queries, ALL, moves[j]) for j in range(4)])
    doc_parts = [passages] + [
        lax.ppermute(passages, "dim", [(i, (i + k) % 4) for i in range(4)]) for k in (1, 2, 3)
    ]
    mine = lax.all_to_all(jnp.broadcast_to(parts[None], (8,) + parts.shape), ("zl", "y"), 0, 0, tiled=True)
    swap = [(0, 1), (1, 0)]
    theirs = lax.ppermute(mine, "core", swap)
    width, doc_cols = 4 * passages.shape[0], passages.shape[1]
    docs = pl.pallas_call(
        docs_kernel,
        out_shape=jax.ShapeDtypeStruct((doc_cols, width), passages.dtype),
        in_specs=vmem(4),
        out_specs=vmem(1)[0],
        name="docs",
    )(*doc_parts)
    rows, slots = cand_ids.shape
    doc_count = doc_cols // DOC_TOK
    cand_scores, send = pl.pallas_call(
        score_kernel,
        out_shape=(
            jax.ShapeDtypeStruct((rows, slots), jnp.float32),
            jax.ShapeDtypeStruct((slots, rows), jnp.float32),
        ),
        in_specs=vmem(5),
        out_specs=tuple(vmem(2)),
        scratch_shapes=[
            pltpu.VMEM((doc_count, queries.shape[1]), jnp.float32),
            pltpu.VMEM((rows, doc_count), jnp.float32),
        ],
        name="score",
    )(docs, mine, theirs, cand_ids, counts)
    got = lax.ppermute(send, "core", swap)
    lane = lax.broadcasted_iota(jnp.int32, send.shape, 1)
    piece = jnp.where(lane < rows // 2, send, got)
    pieces = lax.all_to_all(
        jnp.broadcast_to(piece[None], (32,) + piece.shape), ("zh", "zl", "y"), 0, 0, tiled=True
    )
    top = pl.pallas_call(
        top_kernel,
        out_shape=jax.ShapeDtypeStruct((rows, rows), jnp.float32),
        in_specs=vmem(1),
        out_specs=vmem(1)[0],
        name="top",
    )(pieces.reshape(-1, 8, rows))
    other = lax.ppermute(top, "core", swap)
    row = lax.broadcasted_iota(jnp.int32, top.shape, 0)
    top_scores = jnp.where((row // (rows // 2)) == lax.axis_index("core"), top, other)[:, :TOPK]
    return (cand_scores, top_scores)


def solution(mesh):
    split = Mesh(mesh.devices.reshape(4, 2, 4, 2, 4), ALL)
    own = P(SHARD, "dim")
    return jax.shard_map(
        shards,
        mesh=split,
        in_specs=(P("dim", SHARD),) * 4,
        out_specs=(P("dim", SHARD), P("dim", None)),
        check_vma=False,
    )
```

```python
import jax
import jax.numpy as jnp
from jax import lax
from jax.experimental import pallas as pl
from jax.experimental.pallas import tpu as pltpu
from jax.sharding import Mesh, PartitionSpec as P

DOC_TOK = 64
QTOK = 32
TOPK = 100
LOWEST = -1e30
SHARD = ("zh", "zl", "y", "core")
ALL = SHARD + ("dim",)


def repeat_kernel(a, b, c, d, near, far, out):
    for i in range(out.shape[0]):
        for j, part in enumerate((a, b, c, d)):
            out[i, j] = part[...]


def score_kernel(d0, d1, d2, d3, qa, qb, ids, counts, cand, send, docs, best, kept, picks):
    core = lax.axis_index("core")
    turn = lax.rem(lax.axis_index("zh") - lax.axis_index("dim") + 4, 4)
    docs_n = best.shape[0]
    sources = qa.shape[0]
    slots = ids.shape[0]
    tile = 512
    per = tile // DOC_TOK
    picks[...] = jnp.transpose(jnp.concatenate([ids[...], jnp.zeros((docs_n - slots, ids.shape[1]), jnp.int32)], axis=0))

    def one(source, q, side, first):
        weights = jnp.concatenate([q[source, lax.rem(turn + k, 4)] for k in range(4)], axis=0)
        for t in range(docs_n // per):
            span = slice(t * tile, (t + 1) * tile)
            if first:
                block = jnp.transpose(jnp.concatenate([d[:, span] for d in (d0, d1, d2, d3)], axis=0))
                docs[span, :] = block
            else:
                block = docs[span, :]
            tokens = jnp.dot(block, weights, preferred_element_type=jnp.float32)
            best[t * per : (t + 1) * per, :] = jnp.max(tokens.reshape(per, DOC_TOK, tokens.shape[1]), axis=1)
        turned = jnp.transpose(best[...])
        mean = jnp.sum(turned.reshape(-1, QTOK, docs_n), axis=1) * (1.0 / QTOK)
        queries = mean.shape[0]
        rows = pl.ds(pl.multiple_of((source * 2 + side) * queries, queries), queries)
        kept[rows, :] = jnp.take_along_axis(mean, picks[rows, :], axis=1)

    one(0, qa, core, True)
    one(0, qb, 1 - core, False)

    def pair(source, carry):
        one(source, qa, core, False)
        one(source, qb, 1 - core, False)
        return carry

    lax.fori_loop(1, sources, pair, 0)
    scores = jnp.transpose(kept[...])[:slots, :]
    live = lax.broadcasted_iota(jnp.int32, scores.shape, 0) < counts[...]
    cand[...] = jnp.where(live, scores, 0.0)
    masked = jnp.where(live, scores, LOWEST)
    for i in range(send.shape[0]):
        send[i] = masked


def exchange(values, i, j):
    a, b = values[i], values[j]
    values[i] = jnp.maximum(a, b)
    values[j] = jnp.minimum(a, b)


def odd_even_merge(values, lo, n, r):
    m = r * 2
    if m < n:
        odd_even_merge(values, lo, n, m)
        odd_even_merge(values, lo + r, n, m)
        for i in range(lo + r, lo + n - r, m):
            exchange(values, i, i + r)
    else:
        exchange(values, lo, lo + r)


def odd_even_sort(values, lo, n):
    if n > 1:
        m = n // 2
        odd_even_sort(values, lo, m)
        odd_even_sort(values, lo + m, m)
        odd_even_merge(values, lo, n, 1)


def clean(values, lo, n):
    if n > 1:
        m = n // 2
        for i in range(m):
            exchange(values, lo + i, lo + i + m)
        clean(values, lo, m)
        clean(values, lo + m, m)


def top_kernel(pieces, falling, rising):
    count = pieces.shape[0]
    values = [pieces[i] for i in range(count)]
    odd_even_sort(values, 0, count)
    for shift in (4, 2, 1):
        other = [pltpu.roll(v, shift, 0) for v in values]
        values = [jnp.maximum(values[i], other[count - 1 - i]) for i in range(count)]
        clean(values, 0, count)
    rows = [v[0:1, :] for v in values]
    falling[...] = jnp.concatenate(rows, axis=0)
    rising[...] = jnp.concatenate(rows[::-1], axis=0)


def merge_kernel(falling, rising, out):
    best = jnp.maximum(falling[...], rising[...])
    count = best.shape[0]
    values = [best[i : i + 8, :] for i in range(0, count, 8)]
    clean(values, 0, len(values))
    row = lax.broadcasted_iota(jnp.int32, values[0].shape, 0)
    for shift in (4, 2, 1):
        upper = (row & shift) == 0
        values = [
            jnp.where(upper, jnp.maximum(v, pltpu.roll(v, 8 - shift, 0)), jnp.minimum(v, pltpu.roll(v, shift, 0)))
            for v in values
        ]
    out[...] = jnp.concatenate(values, axis=0)[: out.shape[0], :]


def vmem(n):
    return [pl.BlockSpec(memory_space=pltpu.VMEM)] * n


def anywhere(n):
    return [pl.BlockSpec(memory_space=pl.ANY)] * n


def shards(queries, passages, cand_ids, counts):
    flat = lambda zh, x: zh * 4 + x
    moves = [[(flat(zh, x), flat((x + j) % 4, zh)) for zh in range(4) for x in range(4)] for j in range(4)]
    parts = [lax.ppermute(queries, ("zh", "dim"), moves[j]) for j in range(4)]
    round_dim = lambda k: lax.ppermute(passages, "dim", [(i, (i + k) % 4) for i in range(4)])
    d1, d3 = round_dim(1), round_dim(3)
    d2 = round_dim(2)
    repeated = pl.pallas_call(
        repeat_kernel,
        out_shape=jax.ShapeDtypeStruct((8, 4) + queries.shape, queries.dtype),
        in_specs=vmem(4) + anywhere(2),
        out_specs=vmem(1)[0],
        name="repeat",
    )(*parts, d1, d3)
    mine = lax.all_to_all(repeated, ("zl", "y"), 0, 0, tiled=True)
    swap = [(0, 1), (1, 0)]
    theirs = lax.ppermute(mine, "core", swap)
    width, doc_cols = 4 * passages.shape[0], passages.shape[1]
    rows, slots = cand_ids.shape
    doc_count = doc_cols // DOC_TOK
    cand_scores, send = pl.pallas_call(
        score_kernel,
        out_shape=(
            jax.ShapeDtypeStruct((slots, rows), jnp.float32),
            jax.ShapeDtypeStruct((32, slots, rows), jnp.float32),
        ),
        in_specs=vmem(8),
        out_specs=tuple(vmem(2)),
        scratch_shapes=[
            pltpu.VMEM((doc_cols, width), passages.dtype),
            pltpu.VMEM((doc_count, queries.shape[1]), jnp.float32),
            pltpu.VMEM((rows, doc_count), jnp.float32),
            pltpu.VMEM((rows, doc_count), jnp.int32),
        ],
        name="score",
    )(passages, d1, d2, d3, mine, theirs, jnp.transpose(cand_ids), jnp.transpose(counts))
    pieces = lax.all_to_all(send, ("zh", "zl", "y"), 0, 0, tiled=True)
    falling, rising = pl.pallas_call(
        top_kernel,
        out_shape=(jax.ShapeDtypeStruct((128, rows), jnp.float32),) * 2,
        in_specs=vmem(1),
        out_specs=tuple(vmem(2)),
        name="top",
    )(pieces.reshape(-1, 8, rows))
    other = lax.ppermute(rising, "core", swap)
    top_scores = pl.pallas_call(
        merge_kernel,
        out_shape=jax.ShapeDtypeStruct((TOPK, rows), jnp.float32),
        in_specs=vmem(2),
        out_specs=vmem(1)[0],
        name="merge",
    )(falling, other)
    return (jnp.transpose(cand_scores), jnp.transpose(top_scores))


def solution(mesh):
    split = Mesh(mesh.devices.reshape(4, 2, 4, 2, 4), ALL)
    return jax.shard_map(
        shards,
        mesh=split,
        in_specs=(P("dim", SHARD),) * 4,
        out_specs=(P("dim", SHARD), P("dim", None)),
        check_vma=False,
    )
```

```python
import jax
import jax.numpy as jnp
from jax import lax
from jax.experimental import pallas as pl
from jax.experimental.pallas import tpu as pltpu
from jax.sharding import Mesh, PartitionSpec as P

DOC_TOK = 64
QTOK = 32
TOPK = 100
MIB = 1 << 20
LOWEST = -1e30
SHARD = ("zh", "zl", "y", "core")
ALL = SHARD + ("dim",)


def repeat_kernel(a, b, c, d, near, far, out):
    for i in range(out.shape[0]):
        for j, part in enumerate((a, b, c, d)):
            out[i, j] = part[...]


def score_kernel(d0, d1, d2, d3, qa, qb, ids, counts, cand, send, docs, best, kept, picks):
    core = lax.axis_index("core")
    turn = lax.rem(lax.axis_index("zh") - lax.axis_index("dim") + 4, 4)
    docs_n = best.shape[0]
    sources = qa.shape[0]
    slots = ids.shape[0]
    tile = 512
    per = tile // DOC_TOK
    picks[...] = jnp.transpose(jnp.concatenate([ids[...], jnp.zeros((docs_n - slots, ids.shape[1]), jnp.int32)], axis=0))

    def one(source, q, side, first):
        weights = jnp.concatenate([q[source, lax.rem(turn + k, 4)] for k in range(4)], axis=0)
        for t in range(docs_n // per):
            span = slice(t * tile, (t + 1) * tile)
            if first:
                block = jnp.transpose(jnp.concatenate([d[:, span] for d in (d0, d1, d2, d3)], axis=0))
                docs[span, :] = block
            else:
                block = docs[span, :]
            tokens = jnp.dot(block, weights, preferred_element_type=jnp.float32)
            best[t * per : (t + 1) * per, :] = jnp.max(tokens.reshape(per, DOC_TOK, tokens.shape[1]), axis=1)
        turned = jnp.transpose(best[...])
        mean = jnp.sum(turned.reshape(-1, QTOK, docs_n), axis=1) * (1.0 / QTOK)
        queries = mean.shape[0]
        rows = pl.ds(pl.multiple_of((source * 2 + side) * queries, queries), queries)
        kept[rows, :] = jnp.take_along_axis(mean, picks[rows, :], axis=1)

    one(0, qa, core, True)
    one(0, qb, 1 - core, False)

    def pair(source, carry):
        one(source, qa, core, False)
        one(source, qb, 1 - core, False)
        return carry

    lax.fori_loop(1, sources, pair, 0)
    scores = jnp.transpose(kept[...])[:slots, :]
    live = lax.broadcasted_iota(jnp.int32, scores.shape, 0) < counts[...]
    cand[...] = jnp.where(live, scores, 0.0)
    masked = jnp.where(live, scores, LOWEST)
    for i in range(send.shape[0]):
        send[i] = masked


def exchange(values, i, j):
    a, b = values[i], values[j]
    values[i] = jnp.maximum(a, b)
    values[j] = jnp.minimum(a, b)


def odd_even_merge(values, lo, n, r):
    m = r * 2
    if m < n:
        odd_even_merge(values, lo, n, m)
        odd_even_merge(values, lo + r, n, m)
        for i in range(lo + r, lo + n - r, m):
            exchange(values, i, i + r)
    else:
        exchange(values, lo, lo + r)


def odd_even_sort(values, lo, n):
    if n > 1:
        m = n // 2
        odd_even_sort(values, lo, m)
        odd_even_sort(values, lo + m, m)
        odd_even_merge(values, lo, n, 1)


def clean(values, lo, n):
    if n > 1:
        m = n // 2
        for i in range(m):
            exchange(values, lo + i, lo + i + m)
        clean(values, lo, m)
        clean(values, lo + m, m)


def top_kernel(pieces, falling, rising):
    count = pieces.shape[0]
    values = [pieces[i] for i in range(count)]
    odd_even_sort(values, 0, count)
    for shift in (4, 2, 1):
        other = [pltpu.roll(v, shift, 0) for v in values]
        values = [jnp.maximum(values[i], other[count - 1 - i]) for i in range(count)]
        clean(values, 0, count)
    rows = [v[0:1, :] for v in values]
    falling[...] = jnp.concatenate(rows, axis=0)
    rising[...] = jnp.concatenate(rows[::-1], axis=0)


def merge_kernel(falling, rising, out):
    best = jnp.maximum(falling[...], rising[...])
    count = best.shape[0]
    values = [best[i : i + 8, :] for i in range(0, count, 8)]
    clean(values, 0, len(values))
    row = lax.broadcasted_iota(jnp.int32, values[0].shape, 0)
    for shift in (4, 2, 1):
        upper = (row & shift) == 0
        values = [
            jnp.where(upper, jnp.maximum(v, pltpu.roll(v, 8 - shift, 0)), jnp.minimum(v, pltpu.roll(v, shift, 0)))
            for v in values
        ]
    out[...] = jnp.concatenate(values, axis=0)[: out.shape[0], :]


def vmem(n):
    return [pl.BlockSpec(memory_space=pltpu.VMEM)] * n


def anywhere(n):
    return [pl.BlockSpec(memory_space=pl.ANY)] * n


def shards(queries, passages, cand_ids, counts):
    flat = lambda zh, x: zh * 4 + x
    moves = [[(flat(zh, x), flat((x + j) % 4, zh)) for zh in range(4) for x in range(4)] for j in range(4)]
    parts = [lax.ppermute(queries, ("zh", "dim"), moves[j]) for j in range(4)]
    round_dim = lambda k: lax.ppermute(passages, "dim", [(i, (i + k) % 4) for i in range(4)])
    d1, d3 = round_dim(1), round_dim(3)
    d2 = round_dim(2)
    repeated = pl.pallas_call(
        repeat_kernel,
        out_shape=jax.ShapeDtypeStruct((8, 4) + queries.shape, queries.dtype),
        in_specs=vmem(4) + anywhere(2),
        out_specs=vmem(1)[0],
        compiler_params=pltpu.CompilerParams(vmem_limit_bytes=4 * MIB),
        name="repeat",
    )(*parts, d1, d3)
    mine = lax.all_to_all(repeated, ("zl", "y"), 0, 0, tiled=True)
    swap = [(0, 1), (1, 0)]
    theirs = lax.ppermute(mine, "core", swap)
    width, doc_cols = 4 * passages.shape[0], passages.shape[1]
    rows, slots = cand_ids.shape
    doc_count = doc_cols // DOC_TOK
    cand_scores, send = pl.pallas_call(
        score_kernel,
        out_shape=(
            jax.ShapeDtypeStruct((slots, rows), jnp.float32),
            jax.ShapeDtypeStruct((32, slots, rows), jnp.float32),
        ),
        in_specs=vmem(8),
        out_specs=tuple(vmem(2)),
        scratch_shapes=[
            pltpu.VMEM((doc_cols, width), passages.dtype),
            pltpu.VMEM((doc_count, queries.shape[1]), jnp.float32),
            pltpu.VMEM((rows, doc_count), jnp.float32),
            pltpu.VMEM((rows, doc_count), jnp.int32),
        ],
        compiler_params=pltpu.CompilerParams(vmem_limit_bytes=24 * MIB),
        name="score",
    )(passages, d1, d2, d3, mine, theirs, jnp.transpose(cand_ids), jnp.transpose(counts))
    pieces = lax.all_to_all(send, ("zh", "zl", "y"), 0, 0, tiled=True)
    falling, rising = pl.pallas_call(
        top_kernel,
        out_shape=(jax.ShapeDtypeStruct((128, rows), jnp.float32),) * 2,
        in_specs=vmem(1),
        out_specs=tuple(vmem(2)),
        compiler_params=pltpu.CompilerParams(vmem_limit_bytes=8 * MIB),
        name="top",
    )(pieces.reshape(-1, 8, rows))
    other = lax.ppermute(rising, "core", swap)
    top_scores = pl.pallas_call(
        merge_kernel,
        out_shape=jax.ShapeDtypeStruct((TOPK, rows), jnp.float32),
        in_specs=vmem(2),
        out_specs=vmem(1)[0],
        compiler_params=pltpu.CompilerParams(vmem_limit_bytes=2 * MIB),
        name="merge",
    )(falling, other)
    return (jnp.transpose(cand_scores), jnp.transpose(top_scores))


def solution(mesh):
    split = Mesh(mesh.devices.reshape(4, 2, 4, 2, 4), ALL)
    return jax.shard_map(
        shards,
        mesh=split,
        in_specs=(P("dim", SHARD),) * 4,
        out_specs=(P("dim", SHARD), P("dim", None)),
        check_vma=False,
    )
```

```python
import jax
import jax.numpy as jnp
from jax import lax
from jax.experimental import pallas as pl
from jax.experimental.pallas import tpu as pltpu
from jax.sharding import Mesh, PartitionSpec as P

DOC_TOK = 64
QTOK = 32
TOPK = 100
MIB = 1 << 20
LOWEST = -1e30
SHARD = ("zh", "zl", "y", "core")
ALL = SHARD + ("dim",)


def hold_kernel(q, near, far, out):
    pass


def prepare_kernel(ids, counts, picks, live):
    slots, rows = ids.shape
    picks[...] = jnp.transpose(jnp.concatenate([ids[...], jnp.zeros((picks.shape[1] - slots, rows), jnp.int32)], axis=0))
    live[...] = (lax.broadcasted_iota(jnp.int32, live.shape, 0) < counts[...]).astype(jnp.int32)


def score_kernel(d0, d1, d2, d3, qa, qb, picks, live, cand, send, docs, best, kept):
    core = lax.axis_index("core")
    turn = lax.rem(lax.axis_index("zh") - lax.axis_index("dim") + 4, 4)
    docs_n = best.shape[0]
    sources = qa.shape[0]
    slots = live.shape[0]
    tile = 512
    per = tile // DOC_TOK

    def one(source, q, side, first):
        weights = jnp.concatenate([q[source, lax.rem(turn + k, 4)] for k in range(4)], axis=0)
        for t in range(docs_n // per):
            span = slice(t * tile, (t + 1) * tile)
            if first:
                block = jnp.transpose(jnp.concatenate([d[:, span] for d in (d0, d1, d2, d3)], axis=0))
                docs[span, :] = block
            else:
                block = docs[span, :]
            tokens = jnp.dot(block, weights, preferred_element_type=jnp.float32)
            best[t * per : (t + 1) * per, :] = jnp.max(tokens.reshape(per, DOC_TOK, tokens.shape[1]), axis=1)
        turned = jnp.transpose(best[...])
        mean = jnp.sum(turned.reshape(-1, QTOK, docs_n), axis=1) * (1.0 / QTOK)
        queries = mean.shape[0]
        rows = pl.ds(pl.multiple_of((source * 2 + side) * queries, queries), queries)
        kept[rows, :] = jnp.take_along_axis(mean, picks[rows, :], axis=1)

    def two(source, first):
        for i in range(2):
            one(source + i, qa, core, first and i == 0)
            one(source + i, qb, 1 - core, False)

    def step(i, carry):
        two(2 * i, False)
        return carry

    two(0, True)
    lax.fori_loop(1, sources // 2, step, 0)
    scores = jnp.transpose(kept[...])[:slots, :]
    alive = live[...] > 0
    cand[...] = jnp.where(alive, scores, 0.0)
    masked = jnp.where(alive, scores, LOWEST)
    send[...] = masked


def exchange(values, i, j):
    a, b = values[i], values[j]
    values[i] = jnp.maximum(a, b)
    values[j] = jnp.minimum(a, b)


def odd_even_merge(values, lo, n, r):
    m = r * 2
    if m < n:
        odd_even_merge(values, lo, n, m)
        odd_even_merge(values, lo + r, n, m)
        for i in range(lo + r, lo + n - r, m):
            exchange(values, i, i + r)
    else:
        exchange(values, lo, lo + r)


def odd_even_sort(values, lo, n):
    if n > 1:
        m = n // 2
        odd_even_sort(values, lo, m)
        odd_even_sort(values, lo + m, m)
        odd_even_merge(values, lo, n, 1)


def clean(values, lo, n):
    if n > 1:
        m = n // 2
        for i in range(m):
            exchange(values, lo + i, lo + i + m)
        clean(values, lo, m)
        clean(values, lo + m, m)


def top_kernel(pieces, falling, rising):
    count = pieces.shape[0]
    values = [pieces[i] for i in range(count)]
    odd_even_sort(values, 0, count)
    for shift in (4, 2, 1):
        other = [pltpu.roll(v, shift, 0) for v in values]
        values = [jnp.maximum(values[i], other[count - 1 - i]) for i in range(count)]
        clean(values, 0, count)
    rows = [v[0:1, :] for v in values]
    falling[...] = jnp.concatenate(rows, axis=0)
    rising[...] = jnp.concatenate(rows[::-1], axis=0)


def merge_kernel(falling, rising, out):
    best = jnp.maximum(falling[...], rising[...])
    count = best.shape[0]
    values = [best[i : i + 8, :] for i in range(0, count, 8)]
    clean(values, 0, len(values))
    row = lax.broadcasted_iota(jnp.int32, values[0].shape, 0)
    for shift in (4, 2, 1):
        upper = (row & shift) == 0
        values = [
            jnp.where(upper, jnp.maximum(v, pltpu.roll(v, 8 - shift, 0)), jnp.minimum(v, pltpu.roll(v, shift, 0)))
            for v in values
        ]
    out[...] = jnp.concatenate(values, axis=0)[: out.shape[0], :]


def vmem(n):
    return [pl.BlockSpec(memory_space=pltpu.VMEM)] * n


def anywhere(n):
    return [pl.BlockSpec(memory_space=pl.ANY)] * n


def shards(queries, passages, cand_ids, counts):
    flat = lambda zh, x: zh * 4 + x
    moves = [[(flat(zh, x), flat((x + j) % 4, zh)) for zh in range(4) for x in range(4)] for j in range(4)]
    parts = [lax.ppermute(queries, ("zh", "dim"), moves[j]) for j in range(4)]
    round_dim = lambda k: lax.ppermute(passages, "dim", [(i, (i + k) % 4) for i in range(4)])
    d1, d3 = round_dim(1), round_dim(3)
    d2 = round_dim(2)
    parts = jnp.stack(parts)
    parts = pl.pallas_call(
        hold_kernel,
        out_shape=jax.ShapeDtypeStruct(parts.shape, parts.dtype),
        in_specs=anywhere(3),
        out_specs=anywhere(1)[0],
        input_output_aliases={0: 0},
        compiler_params=pltpu.CompilerParams(vmem_limit_bytes=MIB),
        name="hold",
    )(parts, d1, d3)
    repeated = jnp.broadcast_to(parts[None], (8,) + parts.shape)
    mine = lax.all_to_all(repeated, ("zl", "y"), 0, 0, tiled=True)
    swap = [(0, 1), (1, 0)]
    theirs = lax.ppermute(mine, "core", swap)
    width, doc_cols = 4 * passages.shape[0], passages.shape[1]
    rows, slots = cand_ids.shape
    doc_count = doc_cols // DOC_TOK
    picks, live = pl.pallas_call(
        prepare_kernel,
        out_shape=(
            jax.ShapeDtypeStruct((rows, doc_count), jnp.int32),
            jax.ShapeDtypeStruct((slots, rows), jnp.int32),
        ),
        in_specs=vmem(2),
        out_specs=tuple(vmem(2)),
        compiler_params=pltpu.CompilerParams(vmem_limit_bytes=MIB),
        name="prepare",
    )(jnp.transpose(cand_ids), jnp.transpose(counts))
    cand_scores, send = pl.pallas_call(
        score_kernel,
        out_shape=(
            jax.ShapeDtypeStruct((slots, rows), jnp.float32),
            jax.ShapeDtypeStruct((slots, rows), jnp.float32),
        ),
        in_specs=vmem(8),
        out_specs=tuple(vmem(2)),
        scratch_shapes=[
            pltpu.VMEM((doc_cols, width), passages.dtype),
            pltpu.VMEM((doc_count, queries.shape[1]), jnp.float32),
            pltpu.VMEM((rows, doc_count), jnp.float32),
        ],
        compiler_params=pltpu.CompilerParams(vmem_limit_bytes=24 * MIB),
        name="score",
    )(passages, d1, d2, d3, mine, theirs, picks, live)
    pieces = lax.all_to_all(jnp.broadcast_to(send[None], (32,) + send.shape), ("zh", "zl", "y"), 0, 0, tiled=True)
    falling, rising = pl.pallas_call(
        top_kernel,
        out_shape=(jax.ShapeDtypeStruct((128, rows), jnp.float32),) * 2,
        in_specs=vmem(1),
        out_specs=tuple(vmem(2)),
        compiler_params=pltpu.CompilerParams(vmem_limit_bytes=8 * MIB),
        name="top",
    )(pieces.reshape(-1, 8, rows))
    other = lax.ppermute(rising, "core", swap)
    top_scores = pl.pallas_call(
        merge_kernel,
        out_shape=jax.ShapeDtypeStruct((TOPK, rows), jnp.float32),
        in_specs=vmem(2),
        out_specs=vmem(1)[0],
        compiler_params=pltpu.CompilerParams(vmem_limit_bytes=2 * MIB),
        name="merge",
    )(falling, other)
    return (jnp.transpose(cand_scores), jnp.transpose(top_scores))


def solution(mesh):
    split = Mesh(mesh.devices.reshape(4, 2, 4, 2, 4), ALL)
    return jax.shard_map(
        shards,
        mesh=split,
        in_specs=(P("dim", SHARD),) * 4,
        out_specs=(P("dim", SHARD), P("dim", None)),
        check_vma=False,
    )
```

```python
import jax
import jax.numpy as jnp
from jax import lax
from jax.experimental import pallas as pl
from jax.experimental.pallas import tpu as pltpu
from jax.sharding import Mesh, PartitionSpec as P

DOC_TOK = 64
QTOK = 32
TOPK = 100
MIB = 1 << 20
LOWEST = -1e30
SHARD = ("zh", "zl", "y", "core")
ALL = SHARD + ("dim",)


def hold_kernel(*refs):
    pass


def prepare_kernel(ids, counts, picks, live):
    slots, rows = ids.shape
    picks[...] = jnp.transpose(jnp.concatenate([ids[...], jnp.zeros((picks.shape[1] - slots, rows), jnp.int32)], axis=0))
    live[...] = (lax.broadcasted_iota(jnp.int32, live.shape, 0) < counts[...]).astype(jnp.int32)


def score_kernel(d0, d1, d2a, d2b, d3, qa, qb, picks, live, cand, send, docs, best, kept):
    core = lax.axis_index("core")
    turn = lax.rem(lax.axis_index("zh") - lax.axis_index("dim") + 4, 4)
    docs_n = best.shape[0]
    sources = qa.shape[0]
    slots = live.shape[0]
    tile = 512
    per = tile // DOC_TOK

    def one(source, q, side, first):
        weights = jnp.concatenate([q[source, lax.rem(turn + k, 4)] for k in range(4)], axis=0)
        for t in range(docs_n // per):
            span = slice(t * tile, (t + 1) * tile)
            if first:
                half = d2a.shape[1]
                inner = slice(t * tile % half, t * tile % half + tile)
                two = (d2a if t * tile < half else d2b)[:, inner]
                block = jnp.transpose(jnp.concatenate([d0[:, span], d1[:, span], two, d3[:, span]], axis=0))
                docs[span, :] = block
            else:
                block = docs[span, :]
            tokens = jnp.dot(block, weights, preferred_element_type=jnp.float32)
            best[t * per : (t + 1) * per, :] = jnp.max(tokens.reshape(per, DOC_TOK, tokens.shape[1]), axis=1)
        turned = jnp.transpose(best[...])
        mean = jnp.sum(turned.reshape(-1, QTOK, docs_n), axis=1) * (1.0 / QTOK)
        queries = mean.shape[0]
        rows = pl.ds(pl.multiple_of((source * 2 + side) * queries, queries), queries)
        kept[rows, :] = jnp.take_along_axis(mean, picks[rows, :], axis=1)

    def two(source, first):
        for i in range(2):
            one(source + i, qa, core, first and i == 0)
            one(source + i, qb, 1 - core, False)

    def step(i, carry):
        two(2 * i, False)
        return carry

    two(0, True)
    lax.fori_loop(1, sources // 2, step, 0)
    scores = jnp.transpose(kept[...])[:slots, :]
    alive = live[...] > 0
    cand[...] = jnp.where(alive, scores, 0.0)
    masked = jnp.where(alive, scores, LOWEST)
    half = masked.shape[1] // 2
    upper, lower = slice(0, slots // 2), slice(slots // 2, slots)
    turned = pltpu.roll(masked, half, 1)
    left = lax.broadcasted_iota(jnp.int32, (slots // 2, masked.shape[1]), 1) < half
    send[0] = jnp.where(left, masked[upper, :], turned[lower, :])
    send[1] = jnp.where(left, turned[upper, :], masked[lower, :])


def exchange(values, i, j):
    a, b = values[i], values[j]
    values[i] = jnp.maximum(a, b)
    values[j] = jnp.minimum(a, b)


def odd_even_merge(values, lo, n, r):
    m = r * 2
    if m < n:
        odd_even_merge(values, lo, n, m)
        odd_even_merge(values, lo + r, n, m)
        for i in range(lo + r, lo + n - r, m):
            exchange(values, i, i + r)
    else:
        exchange(values, lo, lo + r)


def odd_even_sort(values, lo, n):
    if n > 1:
        m = n // 2
        odd_even_sort(values, lo, m)
        odd_even_sort(values, lo + m, m)
        odd_even_merge(values, lo, n, 1)


def clean(values, lo, n):
    if n > 1:
        m = n // 2
        for i in range(m):
            exchange(values, lo + i, lo + i + m)
        clean(values, lo, m)
        clean(values, lo + m, m)


def top_kernel(pieces, falling, rising):
    count = pieces.shape[0]
    values = [pieces[i] for i in range(count)]
    odd_even_sort(values, 0, count)
    values = values + [pltpu.roll(v, 64, 1) for v in values[::-1]]
    count = len(values)
    clean(values, 0, count)
    for shift in (4, 2, 1):
        other = [pltpu.roll(v, shift, 0) for v in values]
        values = [jnp.maximum(values[i], other[count - 1 - i]) for i in range(count)]
        clean(values, 0, count)
    rows = [v[0:1, :] for v in values]
    falling[...] = jnp.concatenate(rows, axis=0)
    rising[...] = jnp.concatenate(rows[::-1], axis=0)


def merge_kernel(falling, rising, out):
    best = jnp.maximum(falling[...], rising[...])
    count = best.shape[0]
    values = [best[i : i + 8, :] for i in range(0, count, 8)]
    clean(values, 0, len(values))
    row = lax.broadcasted_iota(jnp.int32, values[0].shape, 0)
    for shift in (4, 2, 1):
        upper = (row & shift) == 0
        values = [
            jnp.where(upper, jnp.maximum(v, pltpu.roll(v, 8 - shift, 0)), jnp.minimum(v, pltpu.roll(v, shift, 0)))
            for v in values
        ]
    out[...] = jnp.concatenate(values, axis=0)[: out.shape[0], :]


def join_kernel(mine, theirs, out):
    side = lax.broadcasted_iota(jnp.int32, out.shape, 1) // (out.shape[1] // 2)
    rows = out.shape[0]
    out[...] = jnp.where(side == lax.axis_index("zl"), mine[:rows, :], theirs[:rows, :])


def vmem(n):
    return [pl.BlockSpec(memory_space=pltpu.VMEM)] * n


def anywhere(n):
    return [pl.BlockSpec(memory_space=pl.ANY)] * n


def hold(q, *ready):
    return pl.pallas_call(
        hold_kernel,
        out_shape=jax.ShapeDtypeStruct(q.shape, q.dtype),
        in_specs=anywhere(1 + len(ready)),
        out_specs=anywhere(1)[0],
        input_output_aliases={0: 0},
        compiler_params=pltpu.CompilerParams(vmem_limit_bytes=MIB),
        name="hold",
    )(q, *ready)


def shards(queries, passages, cand_ids, counts):
    width, doc_cols = 4 * passages.shape[0], passages.shape[1]
    rows, slots = cand_ids.shape
    doc_count = doc_cols // DOC_TOK
    picks, live = pl.pallas_call(
        prepare_kernel,
        out_shape=(
            jax.ShapeDtypeStruct((rows, doc_count), jnp.int32),
            jax.ShapeDtypeStruct((slots, rows), jnp.int32),
        ),
        in_specs=vmem(2),
        out_specs=tuple(vmem(2)),
        compiler_params=pltpu.CompilerParams(vmem_limit_bytes=MIB),
        name="prepare",
    )(jnp.transpose(cand_ids), jnp.transpose(counts))
    flat = lambda zh, x: zh * 4 + x
    moves = [[(flat(zh, x), flat((x + j) % 4, zh)) for zh in range(4) for x in range(4)] for j in range(4)]
    parts = [lax.ppermute(queries, ("zh", "dim"), moves[j]) for j in range(4)]
    round_dim = lambda array, k: lax.ppermute(array, "dim", [(i, (i + k) % 4) for i in range(4)])
    d1, d3 = round_dim(passages, 1), round_dim(passages, 3)
    half = passages.shape[1] // 2
    d2a, d2b = round_dim(d1[:, :half], 1), round_dim(d3[:, half:], 3)
    parts = jnp.stack(parts)
    parts = hold(parts, d1, d3, picks, live)
    repeated = jnp.broadcast_to(parts[None], (8,) + parts.shape)
    mine = hold(lax.all_to_all(repeated, ("zl", "y"), 0, 0, tiled=True), d2a, d2b)
    swap = [(0, 1), (1, 0)]
    theirs = lax.ppermute(mine, "core", swap)
    cand_scores, send = pl.pallas_call(
        score_kernel,
        out_shape=(
            jax.ShapeDtypeStruct((slots, rows), jnp.float32),
            jax.ShapeDtypeStruct((2, slots // 2, rows), jnp.float32),
        ),
        in_specs=vmem(9),
        out_specs=tuple(vmem(2)),
        scratch_shapes=[
            pltpu.VMEM((doc_cols, width), passages.dtype),
            pltpu.VMEM((doc_count, queries.shape[1]), jnp.float32),
            pltpu.VMEM((rows, doc_count), jnp.float32),
        ],
        compiler_params=pltpu.CompilerParams(vmem_limit_bytes=24 * MIB),
        name="score",
    )(passages, d1, d2a, d2b, d3, mine, theirs, picks, live)
    pieces = jnp.broadcast_to(send[None, :, None], (4, 2, 4) + send.shape[1:]).reshape(32, slots // 2, rows)
    pieces = lax.all_to_all(pieces, ("zh", "zl", "y"), 0, 0, tiled=True)
    falling, rising = pl.pallas_call(
        top_kernel,
        out_shape=(jax.ShapeDtypeStruct((128, rows), jnp.float32),) * 2,
        in_specs=vmem(1),
        out_specs=tuple(vmem(2)),
        compiler_params=pltpu.CompilerParams(vmem_limit_bytes=8 * MIB),
        name="top",
    )(pieces.reshape(-1, 8, rows))
    other = lax.ppermute(rising, "core", swap)
    merged = pl.pallas_call(
        merge_kernel,
        out_shape=jax.ShapeDtypeStruct((104, rows), jnp.float32),
        in_specs=vmem(2),
        out_specs=vmem(1)[0],
        compiler_params=pltpu.CompilerParams(vmem_limit_bytes=2 * MIB),
        name="merge",
    )(falling, other)
    top_scores = pl.pallas_call(
        join_kernel,
        out_shape=jax.ShapeDtypeStruct((TOPK, rows), jnp.float32),
        in_specs=vmem(2),
        out_specs=vmem(1)[0],
        compiler_params=pltpu.CompilerParams(vmem_limit_bytes=2 * MIB),
        name="join",
    )(merged, lax.ppermute(merged, "zl", swap))
    return (jnp.transpose(cand_scores), jnp.transpose(top_scores))


def solution(mesh):
    split = Mesh(mesh.devices.reshape(4, 2, 4, 2, 4), ALL)
    return jax.shard_map(
        shards,
        mesh=split,
        in_specs=(P("dim", SHARD),) * 4,
        out_specs=(P("dim", SHARD), P("dim", None)),
        check_vma=False,
    )
```

```python
import jax
import jax.numpy as jnp
from jax import lax
from jax.experimental import pallas as pl
from jax.experimental.pallas import tpu as pltpu
from jax.sharding import Mesh, PartitionSpec as P

DOC_TOK = 64
QTOK = 32
TOPK = 100
MIB = 1 << 20
LOWEST = -1e30
SHARD = ("zh", "zl", "y", "core")
ALL = SHARD + ("dim",)


def hold_kernel(*refs):
    pass


def prepare_kernel(ids, counts, picks, live):
    slots, rows = ids.shape
    picks[...] = jnp.transpose(jnp.concatenate([ids[...], jnp.zeros((picks.shape[1] - slots, rows), jnp.int32)], axis=0))
    live[...] = (lax.broadcasted_iota(jnp.int32, live.shape, 0) < counts[...]).astype(jnp.int32)


def score_queries(passages, qa, qb, zl, picks, docs, best, kept):
    d0, d1, d2a, d2b, d3 = passages
    core = lax.axis_index("core")
    turn = lax.rem(lax.axis_index("zh") - lax.axis_index("dim") + 4, 4)
    docs_n = best.shape[0]
    tile = 512
    per = tile // DOC_TOK

    def one(y, q, side, first):
        weights = jnp.concatenate([q[y, lax.rem(turn + k, 4)] for k in range(4)], axis=0)
        for t in range(docs_n // per):
            span = slice(t * tile, (t + 1) * tile)
            if first:
                half = d2a.shape[1]
                inner = slice(t * tile % half, t * tile % half + tile)
                two = (d2a if t * tile < half else d2b)[:, inner]
                block = jnp.transpose(jnp.concatenate([d0[:, span], d1[:, span], two, d3[:, span]], axis=0))
                docs[span, :] = block
            else:
                block = docs[span, :]
            tokens = jnp.dot(block, weights, preferred_element_type=jnp.float32)
            best[t * per : (t + 1) * per, :] = jnp.max(tokens.reshape(per, DOC_TOK, tokens.shape[1]), axis=1)
        turned = jnp.transpose(best[...])
        mean = jnp.sum(turned.reshape(-1, QTOK, docs_n), axis=1) * (1.0 / QTOK)
        queries = mean.shape[0]
        row = (y * 2 + side) * queries
        chosen = picks[pl.ds(pl.multiple_of(zl * kept.shape[0] + row, queries), queries), :]
        kept[pl.ds(pl.multiple_of(row, queries), queries), :] = jnp.take_along_axis(mean, chosen, axis=1)

    def two(y, first):
        for i in range(2):
            one(y + i, qa, core, first and i == 0)
            one(y + i, qb, 1 - core, False)

    two(0, True)
    two(2, False)


def near_kernel(d0, d1, d2a, d2b, d3, qa, qb, picks, kept, docs, best):
    score_queries((d0, d1, d2a, d2b, d3), qa, qb, lax.axis_index("zl"), picks, docs, best, kept)


def far_kernel(d0, d1, d2a, d2b, d3, qa, qb, picks, near, live, cand, send, docs, best, kept):
    zl = lax.axis_index("zl")
    slots = live.shape[0]
    score_queries((d0, d1, d2a, d2b, d3), qa, qb, 1 - zl, picks, docs, best, kept)
    a, b = near[...], kept[...]
    scores = jnp.concatenate([jnp.where(zl == 0, a, b), jnp.where(zl == 0, b, a)], axis=0)
    scores = jnp.transpose(scores)[:slots, :]
    alive = live[...] > 0
    cand[...] = jnp.where(alive, scores, 0.0)
    masked = jnp.where(alive, scores, LOWEST)
    half = masked.shape[1] // 2
    upper, lower = slice(0, slots // 2), slice(slots // 2, slots)
    turned = pltpu.roll(masked, half, 1)
    left = lax.broadcasted_iota(jnp.int32, (slots // 2, masked.shape[1]), 1) < half
    send[0] = jnp.where(left, masked[upper, :], turned[lower, :])
    send[1] = jnp.where(left, turned[upper, :], masked[lower, :])


def exchange(values, i, j):
    a, b = values[i], values[j]
    values[i] = jnp.maximum(a, b)
    values[j] = jnp.minimum(a, b)


def odd_even_merge(values, lo, n, r):
    m = r * 2
    if m < n:
        odd_even_merge(values, lo, n, m)
        odd_even_merge(values, lo + r, n, m)
        for i in range(lo + r, lo + n - r, m):
            exchange(values, i, i + r)
    else:
        exchange(values, lo, lo + r)


def odd_even_sort(values, lo, n):
    if n > 1:
        m = n // 2
        odd_even_sort(values, lo, m)
        odd_even_sort(values, lo + m, m)
        odd_even_merge(values, lo, n, 1)


def clean(values, lo, n):
    if n > 1:
        m = n // 2
        for i in range(m):
            exchange(values, lo + i, lo + i + m)
        clean(values, lo, m)
        clean(values, lo + m, m)


def top_kernel(pieces, falling, rising):
    count = pieces.shape[0]
    values = [pieces[i] for i in range(count)]
    odd_even_sort(values, 0, count)
    values = values + [pltpu.roll(v, 64, 1) for v in values[::-1]]
    count = len(values)
    clean(values, 0, count)
    for shift in (4, 2, 1):
        other = [pltpu.roll(v, shift, 0) for v in values]
        values = [jnp.maximum(values[i], other[count - 1 - i]) for i in range(count)]
        clean(values, 0, count)
    rows = [v[0:1, :] for v in values]
    falling[...] = jnp.concatenate(rows, axis=0)
    rising[...] = jnp.concatenate(rows[::-1], axis=0)


def merge_kernel(falling, rising, out):
    best = jnp.maximum(falling[...], rising[...])
    count = best.shape[0]
    values = [best[i : i + 8, :] for i in range(0, count, 8)]
    clean(values, 0, len(values))
    row = lax.broadcasted_iota(jnp.int32, values[0].shape, 0)
    for shift in (4, 2, 1):
        upper = (row & shift) == 0
        values = [
            jnp.where(upper, jnp.maximum(v, pltpu.roll(v, 8 - shift, 0)), jnp.minimum(v, pltpu.roll(v, shift, 0)))
            for v in values
        ]
    out[...] = jnp.concatenate(values, axis=0)[: out.shape[0], :]


def join_kernel(mine, theirs, out):
    side = lax.broadcasted_iota(jnp.int32, out.shape, 1) // (out.shape[1] // 2)
    rows = out.shape[0]
    out[...] = jnp.where(side == lax.axis_index("zl"), mine[:rows, :], theirs[:rows, :])


def vmem(n):
    return [pl.BlockSpec(memory_space=pltpu.VMEM)] * n


def anywhere(n):
    return [pl.BlockSpec(memory_space=pl.ANY)] * n


def hold(q, *ready):
    return pl.pallas_call(
        hold_kernel,
        out_shape=jax.ShapeDtypeStruct(q.shape, q.dtype),
        in_specs=anywhere(1 + len(ready)),
        out_specs=anywhere(1)[0],
        input_output_aliases={0: 0},
        compiler_params=pltpu.CompilerParams(vmem_limit_bytes=MIB),
        name="hold",
    )(q, *ready)


def shards(queries, passages, cand_ids, counts):
    width, doc_cols = 4 * passages.shape[0], passages.shape[1]
    rows, slots = cand_ids.shape
    doc_count = doc_cols // DOC_TOK
    picks, live = pl.pallas_call(
        prepare_kernel,
        out_shape=(
            jax.ShapeDtypeStruct((rows, doc_count), jnp.int32),
            jax.ShapeDtypeStruct((slots, rows), jnp.int32),
        ),
        in_specs=vmem(2),
        out_specs=tuple(vmem(2)),
        compiler_params=pltpu.CompilerParams(vmem_limit_bytes=MIB),
        name="prepare",
    )(jnp.transpose(cand_ids), jnp.transpose(counts))
    flat = lambda zh, x: zh * 4 + x
    moves = [[(flat(zh, x), flat((x + j) % 4, zh)) for zh in range(4) for x in range(4)] for j in range(4)]
    parts = [lax.ppermute(queries, ("zh", "dim"), moves[j]) for j in range(4)]
    round_dim = lambda array, k: lax.ppermute(array, "dim", [(i, (i + k) % 4) for i in range(4)])
    d1, d3 = round_dim(passages, 1), round_dim(passages, 3)
    half = passages.shape[1] // 2
    d2a, d2b = round_dim(d1[:, :half], 1), round_dim(d3[:, half:], 3)
    parts = jnp.stack(parts)
    parts = hold(parts, d1, d3, picks, live)
    repeated = jnp.broadcast_to(parts[None], (4,) + parts.shape)
    swap = [(0, 1), (1, 0)]
    mine = hold(lax.all_to_all(repeated, "y", 0, 0, tiled=True), d2a, d2b)
    theirs = lax.ppermute(mine, "core", swap)
    mine_far = lax.ppermute(mine, "zl", swap)
    cost = pl.CostEstimate(flops=rows * QTOK * doc_cols * width, bytes_accessed=1 << 20, transcendentals=0)
    scratch = [
        pltpu.VMEM((doc_cols, width), passages.dtype),
        pltpu.VMEM((doc_count, queries.shape[1]), jnp.float32),
    ]
    all_passages = (passages, d1, d2a, d2b, d3)
    near = pl.pallas_call(
        near_kernel,
        out_shape=jax.ShapeDtypeStruct((rows // 2, doc_count), jnp.float32),
        in_specs=vmem(8),
        out_specs=vmem(1)[0],
        scratch_shapes=scratch,
        cost_estimate=cost,
        compiler_params=pltpu.CompilerParams(vmem_limit_bytes=20 * MIB),
        name="near",
    )(*all_passages, mine, theirs, picks)
    mine_far = hold(mine_far, near)
    theirs_far = lax.ppermute(mine_far, "core", swap)
    cand_scores, send = pl.pallas_call(
        far_kernel,
        out_shape=(
            jax.ShapeDtypeStruct((slots, rows), jnp.float32),
            jax.ShapeDtypeStruct((2, slots // 2, rows), jnp.float32),
        ),
        in_specs=vmem(10),
        out_specs=tuple(vmem(2)),
        scratch_shapes=scratch + [pltpu.VMEM((rows // 2, doc_count), jnp.float32)],
        cost_estimate=cost,
        compiler_params=pltpu.CompilerParams(vmem_limit_bytes=20 * MIB),
        name="far",
    )(*all_passages, mine_far, theirs_far, picks, near, live)
    pieces = jnp.broadcast_to(send[None, :, None], (4, 2, 4) + send.shape[1:]).reshape(32, slots // 2, rows)
    pieces = lax.all_to_all(pieces, ("zh", "zl", "y"), 0, 0, tiled=True)
    falling, rising = pl.pallas_call(
        top_kernel,
        out_shape=(jax.ShapeDtypeStruct((128, rows), jnp.float32),) * 2,
        in_specs=vmem(1),
        out_specs=tuple(vmem(2)),
        compiler_params=pltpu.CompilerParams(vmem_limit_bytes=8 * MIB),
        name="top",
    )(pieces.reshape(-1, 8, rows))
    other = lax.ppermute(rising, "core", swap)
    merged = pl.pallas_call(
        merge_kernel,
        out_shape=jax.ShapeDtypeStruct((104, rows), jnp.float32),
        in_specs=vmem(2),
        out_specs=vmem(1)[0],
        compiler_params=pltpu.CompilerParams(vmem_limit_bytes=2 * MIB),
        name="merge",
    )(falling, other)
    top_scores = pl.pallas_call(
        join_kernel,
        out_shape=jax.ShapeDtypeStruct((TOPK, rows), jnp.float32),
        in_specs=vmem(2),
        out_specs=vmem(1)[0],
        compiler_params=pltpu.CompilerParams(vmem_limit_bytes=2 * MIB),
        name="join",
    )(merged, lax.ppermute(merged, "zl", swap))
    return (jnp.transpose(cand_scores), jnp.transpose(top_scores))


def solution(mesh):
    split = Mesh(mesh.devices.reshape(4, 2, 4, 2, 4), ALL)
    return jax.shard_map(
        shards,
        mesh=split,
        in_specs=(P("dim", SHARD),) * 4,
        out_specs=(P("dim", SHARD), P("dim", None)),
        check_vma=False,
    )
```

```python
import jax
import jax.numpy as jnp
from jax import lax
from jax.experimental import pallas as pl
from jax.experimental.pallas import tpu as pltpu
from jax.sharding import Mesh, PartitionSpec as P

DOC_TOK = 64
QTOK = 32
TOPK = 100
MIB = 1 << 20
LOWEST = -1e30
SHARD = ("zh", "zl", "y", "core")
ALL = SHARD + ("dim",)


def hold_kernel(*refs):
    pass


def prepare_kernel(ids, counts, picks, live):
    slots, rows = ids.shape
    picks[...] = jnp.transpose(jnp.concatenate([ids[...], jnp.zeros((picks.shape[1] - slots, rows), jnp.int32)], axis=0))
    live[...] = (lax.broadcasted_iota(jnp.int32, live.shape, 0) < counts[...]).astype(jnp.int32)


def score_queries(passages, sources, zl, picks, docs, best, kept):
    d0, d1, d2a, d2b, d3 = passages
    turn = lax.rem(lax.axis_index("zh") - lax.axis_index("dim") + 4, 4)
    docs_n = best.shape[0]
    tile = 512
    per = tile // DOC_TOK

    def one(y, q, side, first):
        weights = jnp.concatenate([q[y, lax.rem(turn + k, 4)] for k in range(4)], axis=0)
        for t in range(docs_n // per):
            span = slice(t * tile, (t + 1) * tile)
            if first:
                half = d2a.shape[1]
                inner = slice(t * tile % half, t * tile % half + tile)
                two = (d2a if t * tile < half else d2b)[:, inner]
                block = jnp.transpose(jnp.concatenate([d0[:, span], d1[:, span], two, d3[:, span]], axis=0))
                docs[span, :] = block
            else:
                block = docs[span, :]
            tokens = jnp.dot(block, weights, preferred_element_type=jnp.float32)
            best[t * per : (t + 1) * per, :] = jnp.max(tokens.reshape(per, DOC_TOK, tokens.shape[1]), axis=1)
        turned = jnp.transpose(best[...])
        mean = jnp.sum(turned.reshape(-1, QTOK, docs_n), axis=1) * (1.0 / QTOK)
        queries = mean.shape[0]
        row = (y * 2 + side) * queries
        chosen = picks[pl.ds(pl.multiple_of(zl * kept.shape[0] + row, queries), queries), :]
        kept[pl.ds(pl.multiple_of(row, queries), queries), :] = jnp.take_along_axis(mean, chosen, axis=1)

    first = True
    for y in range(sources[0][0].shape[0]):
        for q, side in sources:
            one(y, q, side, first)
            first = False


def near_kernel(d0, d1, d2a, d2b, d3, qa, qb, picks, kept, docs, best):
    core = lax.axis_index("core")
    sources = ((qa, core), (qb, 1 - core))
    score_queries((d0, d1, d2a, d2b, d3), sources, lax.axis_index("zl"), picks, docs, best, kept)


def far_kernel(d0, d1, d2a, d2b, d3, qa, picks, kept, docs, best):
    kept[...] = jnp.zeros_like(kept)
    sources = ((qa, lax.axis_index("core")),)
    score_queries((d0, d1, d2a, d2b, d3), sources, 1 - lax.axis_index("zl"), picks, docs, best, kept)


def last_kernel(d0, d1, d2a, d2b, d3, qb, picks, near, far, live, cand, send, docs, best, kept):
    core, zl = lax.axis_index("core"), lax.axis_index("zl")
    slots = live.shape[0]
    score_queries((d0, d1, d2a, d2b, d3), ((qb, 1 - core),), 1 - zl, picks, docs, best, kept)
    group = lax.broadcasted_iota(jnp.int32, kept.shape, 0) // 8
    a, b = near[...], jnp.where(lax.rem(group, 2) == core, far[...], kept[...])
    scores = jnp.concatenate([jnp.where(zl == 0, a, b), jnp.where(zl == 0, b, a)], axis=0)
    scores = jnp.transpose(scores)[:slots, :]
    alive = live[...] > 0
    cand[...] = jnp.where(alive, scores, 0.0)
    masked = jnp.where(alive, scores, LOWEST)
    half = masked.shape[1] // 2
    upper, lower = slice(0, slots // 2), slice(slots // 2, slots)
    turned = pltpu.roll(masked, half, 1)
    left = lax.broadcasted_iota(jnp.int32, (slots // 2, masked.shape[1]), 1) < half
    send[0] = jnp.where(left, masked[upper, :], turned[lower, :])
    send[1] = jnp.where(left, turned[upper, :], masked[lower, :])


def exchange(values, i, j):
    a, b = values[i], values[j]
    values[i] = jnp.maximum(a, b)
    values[j] = jnp.minimum(a, b)


def odd_even_merge(values, lo, n, r):
    m = r * 2
    if m < n:
        odd_even_merge(values, lo, n, m)
        odd_even_merge(values, lo + r, n, m)
        for i in range(lo + r, lo + n - r, m):
            exchange(values, i, i + r)
    else:
        exchange(values, lo, lo + r)


def odd_even_sort(values, lo, n):
    if n > 1:
        m = n // 2
        odd_even_sort(values, lo, m)
        odd_even_sort(values, lo + m, m)
        odd_even_merge(values, lo, n, 1)


def clean(values, lo, n):
    if n > 1:
        m = n // 2
        for i in range(m):
            exchange(values, lo + i, lo + i + m)
        clean(values, lo, m)
        clean(values, lo + m, m)


def top_kernel(pieces, falling, rising):
    count = pieces.shape[0]
    values = [pieces[i] for i in range(count)]
    odd_even_sort(values, 0, count)
    values = values + [pltpu.roll(v, 64, 1) for v in values[::-1]]
    count = len(values)
    clean(values, 0, count)
    for shift in (4, 2, 1):
        other = [pltpu.roll(v, shift, 0) for v in values]
        values = [jnp.maximum(values[i], other[count - 1 - i]) for i in range(count)]
        clean(values, 0, count)
    rows = [v[0:1, :] for v in values]
    falling[...] = jnp.concatenate(rows, axis=0)
    rising[...] = jnp.concatenate(rows[::-1], axis=0)


def merge_kernel(falling, rising, out):
    best = jnp.maximum(falling[...], rising[...])
    count = best.shape[0]
    values = [best[i : i + 8, :] for i in range(0, count, 8)]
    clean(values, 0, len(values))
    row = lax.broadcasted_iota(jnp.int32, values[0].shape, 0)
    for shift in (4, 2, 1):
        upper = (row & shift) == 0
        values = [
            jnp.where(upper, jnp.maximum(v, pltpu.roll(v, 8 - shift, 0)), jnp.minimum(v, pltpu.roll(v, shift, 0)))
            for v in values
        ]
    out[...] = jnp.concatenate(values, axis=0)[: out.shape[0], :]


def join_kernel(mine, theirs, out):
    side = lax.broadcasted_iota(jnp.int32, out.shape, 1) // (out.shape[1] // 2)
    rows = out.shape[0]
    out[...] = jnp.where(side == lax.axis_index("zl"), mine[:rows, :], theirs[:rows, :])


def vmem(n):
    return [pl.BlockSpec(memory_space=pltpu.VMEM)] * n


def anywhere(n):
    return [pl.BlockSpec(memory_space=pl.ANY)] * n


def hold(q, *ready):
    return pl.pallas_call(
        hold_kernel,
        out_shape=jax.ShapeDtypeStruct(q.shape, q.dtype),
        in_specs=anywhere(1 + len(ready)),
        out_specs=anywhere(1)[0],
        input_output_aliases={0: 0},
        compiler_params=pltpu.CompilerParams(vmem_limit_bytes=MIB),
        name="hold",
    )(q, *ready)


def shards(queries, passages, cand_ids, counts):
    width, doc_cols = 4 * passages.shape[0], passages.shape[1]
    rows, slots = cand_ids.shape
    doc_count = doc_cols // DOC_TOK
    picks, live = pl.pallas_call(
        prepare_kernel,
        out_shape=(
            jax.ShapeDtypeStruct((rows, doc_count), jnp.int32),
            jax.ShapeDtypeStruct((slots, rows), jnp.int32),
        ),
        in_specs=vmem(2),
        out_specs=tuple(vmem(2)),
        compiler_params=pltpu.CompilerParams(vmem_limit_bytes=MIB),
        name="prepare",
    )(jnp.transpose(cand_ids), jnp.transpose(counts))
    flat = lambda zh, x: zh * 4 + x
    moves = [[(flat(zh, x), flat((x + j) % 4, zh)) for zh in range(4) for x in range(4)] for j in range(4)]
    parts = [lax.ppermute(queries, ("zh", "dim"), moves[j]) for j in range(4)]
    round_dim = lambda array, k: lax.ppermute(array, "dim", [(i, (i + k) % 4) for i in range(4)])
    d1, d3 = round_dim(passages, 1), round_dim(passages, 3)
    half = passages.shape[1] // 2
    d2a, d2b = round_dim(d1[:, :half], 1), round_dim(d3[:, half:], 3)
    parts = jnp.stack(parts)
    parts = hold(parts, d1, d3, picks, live)
    repeated = jnp.broadcast_to(parts[None], (4,) + parts.shape)
    swap = [(0, 1), (1, 0)]
    mine = hold(lax.all_to_all(repeated, "y", 0, 0, tiled=True), d2a, d2b)
    theirs = lax.ppermute(mine, "core", swap)
    mine_far = lax.ppermute(mine, "zl", swap)
    cost = pl.CostEstimate(flops=rows * QTOK * doc_cols * width, bytes_accessed=1 << 20, transcendentals=0)
    scratch = [
        pltpu.VMEM((doc_cols, width), passages.dtype),
        pltpu.VMEM((doc_count, queries.shape[1]), jnp.float32),
    ]
    all_passages = (passages, d1, d2a, d2b, d3)
    near = pl.pallas_call(
        near_kernel,
        out_shape=jax.ShapeDtypeStruct((rows // 2, doc_count), jnp.float32),
        in_specs=vmem(8),
        out_specs=vmem(1)[0],
        scratch_shapes=scratch,
        cost_estimate=cost,
        compiler_params=pltpu.CompilerParams(vmem_limit_bytes=20 * MIB),
        name="near",
    )(*all_passages, mine, theirs, picks)
    mine_far = hold(mine_far, near)
    theirs_far = lax.ppermute(mine_far, "core", swap)
    less = pl.CostEstimate(flops=cost.flops // 2, bytes_accessed=1 << 20, transcendentals=0)
    far = pl.pallas_call(
        far_kernel,
        out_shape=jax.ShapeDtypeStruct((rows // 2, doc_count), jnp.float32),
        in_specs=vmem(7),
        out_specs=vmem(1)[0],
        scratch_shapes=scratch,
        cost_estimate=less,
        compiler_params=pltpu.CompilerParams(vmem_limit_bytes=20 * MIB),
        name="far",
    )(*all_passages, mine_far, picks)
    cand_scores, send = pl.pallas_call(
        last_kernel,
        out_shape=(
            jax.ShapeDtypeStruct((slots, rows), jnp.float32),
            jax.ShapeDtypeStruct((2, slots // 2, rows), jnp.float32),
        ),
        in_specs=vmem(10),
        out_specs=tuple(vmem(2)),
        scratch_shapes=scratch + [pltpu.VMEM((rows // 2, doc_count), jnp.float32)],
        cost_estimate=less,
        compiler_params=pltpu.CompilerParams(vmem_limit_bytes=20 * MIB),
        name="last",
    )(*all_passages, theirs_far, picks, near, far, live)
    pieces = jnp.broadcast_to(send[None, :, None], (4, 2, 4) + send.shape[1:]).reshape(32, slots // 2, rows)
    pieces = lax.all_to_all(pieces, ("zh", "zl", "y"), 0, 0, tiled=True)
    falling, rising = pl.pallas_call(
        top_kernel,
        out_shape=(jax.ShapeDtypeStruct((128, rows), jnp.float32),) * 2,
        in_specs=vmem(1),
        out_specs=tuple(vmem(2)),
        compiler_params=pltpu.CompilerParams(vmem_limit_bytes=8 * MIB),
        name="top",
    )(pieces.reshape(-1, 8, rows))
    other = lax.ppermute(rising, "core", swap)
    merged = pl.pallas_call(
        merge_kernel,
        out_shape=jax.ShapeDtypeStruct((104, rows), jnp.float32),
        in_specs=vmem(2),
        out_specs=vmem(1)[0],
        compiler_params=pltpu.CompilerParams(vmem_limit_bytes=2 * MIB),
        name="merge",
    )(falling, other)
    top_scores = pl.pallas_call(
        join_kernel,
        out_shape=jax.ShapeDtypeStruct((TOPK, rows), jnp.float32),
        in_specs=vmem(2),
        out_specs=vmem(1)[0],
        compiler_params=pltpu.CompilerParams(vmem_limit_bytes=2 * MIB),
        name="join",
    )(merged, lax.ppermute(merged, "zl", swap))
    return (jnp.transpose(cand_scores), jnp.transpose(top_scores))


def solution(mesh):
    split = Mesh(mesh.devices.reshape(4, 2, 4, 2, 4), ALL)
    return jax.shard_map(
        shards,
        mesh=split,
        in_specs=(P("dim", SHARD),) * 4,
        out_specs=(P("dim", SHARD), P("dim", None)),
        check_vma=False,
    )
```

```python
import jax
import jax.numpy as jnp
from jax import lax
from jax.experimental import pallas as pl
from jax.experimental.pallas import tpu as pltpu
from jax.sharding import Mesh, PartitionSpec as P

DOC_TOK = 64
QTOK = 32
TOPK = 100
MIB = 1 << 20
LOWEST = -1e30
SHARD = ("zh", "zl", "y", "core")
ALL = SHARD + ("dim",)


def hold_kernel(*refs):
    pass


def prepare_kernel(ids, counts, picks, live):
    slots, rows = ids.shape
    picks[...] = jnp.transpose(jnp.concatenate([ids[...], jnp.zeros((picks.shape[1] - slots, rows), jnp.int32)], axis=0))
    live[...] = (lax.broadcasted_iota(jnp.int32, live.shape, 0) < counts[...]).astype(jnp.int32)


def score_queries(passages, sources, zl, picks, docs, best, kept):
    d0, d1, d2a, d2b, d3 = passages
    turn = lax.rem(lax.axis_index("zh") - lax.axis_index("dim") + 4, 4)
    docs_n = best.shape[0]
    tile = 512
    per = tile // DOC_TOK

    def one(y, q, side, first):
        weights = jnp.concatenate([q[y, lax.rem(turn + k, 4)] for k in range(4)], axis=0)
        for t in range(docs_n // per):
            span = slice(t * tile, (t + 1) * tile)
            if first:
                half = d2a.shape[1]
                inner = slice(t * tile % half, t * tile % half + tile)
                two = (d2a if t * tile < half else d2b)[:, inner]
                block = jnp.transpose(jnp.concatenate([d0[:, span], d1[:, span], two, d3[:, span]], axis=0))
                docs[span, :] = block
            else:
                block = docs[span, :]
            tokens = jnp.dot(block, weights, preferred_element_type=jnp.float32)
            best[t * per : (t + 1) * per, :] = jnp.max(tokens.reshape(per, DOC_TOK, tokens.shape[1]), axis=1)
        turned = jnp.transpose(best[...])
        mean = jnp.sum(turned.reshape(-1, QTOK, docs_n), axis=1) * (1.0 / QTOK)
        queries = mean.shape[0]
        row = (y * 2 + side) * queries
        chosen = picks[pl.ds(pl.multiple_of(zl * kept.shape[0] + row, queries), queries), :]
        kept[pl.ds(pl.multiple_of(row, queries), queries), :] = jnp.take_along_axis(mean, chosen, axis=1)

    first = True
    for y in range(sources[0][0].shape[0]):
        for q, side in sources:
            one(y, q, side, first)
            first = False


def near_kernel(d0, d1, d2a, d2b, d3, qa, qb, picks, kept, docs, best):
    core = lax.axis_index("core")
    sources = ((qa, core), (qb, 1 - core))
    score_queries((d0, d1, d2a, d2b, d3), sources, lax.axis_index("zl"), picks, docs, best, kept)


def far_kernel(d0, d1, d2a, d2b, d3, qa, picks, kept, docs, best):
    kept[...] = jnp.zeros_like(kept)
    sources = ((qa, lax.axis_index("core")),)
    score_queries((d0, d1, d2a, d2b, d3), sources, 1 - lax.axis_index("zl"), picks, docs, best, kept)


def last_kernel(d0, d1, d2a, d2b, d3, qb, picks, near, far, live, cand, send, docs, best, kept):
    core, zl = lax.axis_index("core"), lax.axis_index("zl")
    slots = live.shape[0]
    score_queries((d0, d1, d2a, d2b, d3), ((qb, 1 - core),), 1 - zl, picks, docs, best, kept)
    group = lax.broadcasted_iota(jnp.int32, kept.shape, 0) // 8
    a, b = near[...], jnp.where(lax.rem(group, 2) == core, far[...], kept[...])
    scores = jnp.concatenate([jnp.where(zl == 0, a, b), jnp.where(zl == 0, b, a)], axis=0)
    scores = jnp.transpose(scores)[:slots, :]
    alive = live[...] > 0
    cand[...] = jnp.where(alive, scores, 0.0)
    masked = jnp.where(alive, scores, LOWEST)
    half = masked.shape[1] // 2
    upper, lower = slice(0, slots // 2), slice(slots // 2, slots)
    turned = pltpu.roll(masked, half, 1)
    left = lax.broadcasted_iota(jnp.int32, (slots // 2, masked.shape[1]), 1) < half
    send[0] = jnp.where(left, masked[upper, :], turned[lower, :])
    send[1] = jnp.where(left, turned[upper, :], masked[lower, :])


def exchange(values, i, j):
    a, b = values[i], values[j]
    values[i] = jnp.maximum(a, b)
    values[j] = jnp.minimum(a, b)


def odd_even_merge(values, lo, n, r):
    m = r * 2
    if m < n:
        odd_even_merge(values, lo, n, m)
        odd_even_merge(values, lo + r, n, m)
        for i in range(lo + r, lo + n - r, m):
            exchange(values, i, i + r)
    else:
        exchange(values, lo, lo + r)


def odd_even_sort(values, lo, n):
    if n > 1:
        m = n // 2
        odd_even_sort(values, lo, m)
        odd_even_sort(values, lo + m, m)
        odd_even_merge(values, lo, n, 1)


def clean(values, lo, n):
    if n > 1:
        m = n // 2
        for i in range(m):
            exchange(values, lo + i, lo + i + m)
        clean(values, lo, m)
        clean(values, lo + m, m)


def top_kernel(pieces, falling, rising):
    count = pieces.shape[0]
    values = [pieces[i] for i in range(count)]
    odd_even_sort(values, 0, count)
    values = values + [pltpu.roll(v, 64, 1) for v in values[::-1]]
    count = len(values)
    clean(values, 0, count)
    for shift in (4, 2, 1):
        other = [pltpu.roll(v, shift, 0) for v in values]
        values = [jnp.maximum(values[i], other[count - 1 - i]) for i in range(count)]
        clean(values, 0, count)
    rows = [v[0:1, :] for v in values]
    falling[...] = jnp.concatenate(rows, axis=0)
    rising[...] = jnp.concatenate(rows[::-1], axis=0)


def merge_kernel(falling, rising, out):
    best = jnp.maximum(falling[...], rising[...])
    count = best.shape[0]
    values = [best[i : i + 8, :] for i in range(0, count, 8)]
    clean(values, 0, len(values))
    row = lax.broadcasted_iota(jnp.int32, values[0].shape, 0)
    for shift in (4, 2, 1):
        upper = (row & shift) == 0
        values = [
            jnp.where(upper, jnp.maximum(v, pltpu.roll(v, 8 - shift, 0)), jnp.minimum(v, pltpu.roll(v, shift, 0)))
            for v in values
        ]
    out[...] = jnp.concatenate(values, axis=0)[: out.shape[0], :]


def join_kernel(mine, theirs, out):
    side = lax.broadcasted_iota(jnp.int32, out.shape, 1) // (out.shape[1] // 2)
    rows = out.shape[0]
    out[...] = jnp.where(side == lax.axis_index("zl"), mine[:rows, :], theirs[:rows, :])


def vmem(n):
    return [pl.BlockSpec(memory_space=pltpu.VMEM)] * n


def anywhere(n):
    return [pl.BlockSpec(memory_space=pl.ANY)] * n


def hold(q, *ready):
    return pl.pallas_call(
        hold_kernel,
        out_shape=jax.ShapeDtypeStruct(q.shape, q.dtype),
        in_specs=anywhere(1 + len(ready)),
        out_specs=anywhere(1)[0],
        input_output_aliases={0: 0},
        compiler_params=pltpu.CompilerParams(vmem_limit_bytes=MIB),
        name="hold",
    )(q, *ready)


def shards(queries, passages, cand_ids, counts):
    width, doc_cols = 4 * passages.shape[0], passages.shape[1]
    rows, slots = cand_ids.shape
    doc_count = doc_cols // DOC_TOK
    picks, live = pl.pallas_call(
        prepare_kernel,
        out_shape=(
            jax.ShapeDtypeStruct((rows, doc_count), jnp.int32),
            jax.ShapeDtypeStruct((slots, rows), jnp.int32),
        ),
        in_specs=vmem(2),
        out_specs=tuple(vmem(2)),
        compiler_params=pltpu.CompilerParams(vmem_limit_bytes=MIB),
        name="prepare",
    )(jnp.transpose(cand_ids), jnp.transpose(counts))
    flat = lambda zh, x: zh * 4 + x
    moves = [[(flat(zh, x), flat((x + j) % 4, zh)) for zh in range(4) for x in range(4)] for j in range(4)]
    parts = [lax.ppermute(queries, ("zh", "dim"), moves[j]) for j in range(4)]
    round_dim = lambda array, k: lax.ppermute(array, "dim", [(i, (i + k) % 4) for i in range(4)])
    d1, d3 = round_dim(passages, 1), round_dim(passages, 3)
    half = passages.shape[1] // 2
    d2a, d2b = round_dim(d1[:, :half], 1), round_dim(d3[:, half:], 3)
    parts = jnp.stack(parts)
    parts = hold(parts, d1, d3)
    repeated = jnp.broadcast_to(parts[None], (4,) + parts.shape)
    swap = [(0, 1), (1, 0)]
    mine = hold(lax.all_to_all(repeated, "y", 0, 0, tiled=True), d2a, d2b)
    theirs = lax.ppermute(mine, "core", swap)
    mine_far = lax.ppermute(mine, "zl", swap)
    cost = pl.CostEstimate(flops=rows * QTOK * doc_cols * width, bytes_accessed=1 << 20, transcendentals=0)
    scratch = [
        pltpu.VMEM((doc_cols, width), passages.dtype),
        pltpu.VMEM((doc_count, queries.shape[1]), jnp.float32),
    ]
    all_passages = (passages, d1, d2a, d2b, d3)
    near = pl.pallas_call(
        near_kernel,
        out_shape=jax.ShapeDtypeStruct((rows // 2, doc_count), jnp.float32),
        in_specs=vmem(8),
        out_specs=vmem(1)[0],
        scratch_shapes=scratch,
        cost_estimate=cost,
        compiler_params=pltpu.CompilerParams(vmem_limit_bytes=20 * MIB),
        name="near",
    )(*all_passages, mine, theirs, picks)
    mine_far = hold(mine_far, near)
    theirs_far = lax.ppermute(mine_far, "core", swap)
    less = pl.CostEstimate(flops=cost.flops // 2, bytes_accessed=1 << 20, transcendentals=0)
    far = pl.pallas_call(
        far_kernel,
        out_shape=jax.ShapeDtypeStruct((rows // 2, doc_count), jnp.float32),
        in_specs=vmem(7),
        out_specs=vmem(1)[0],
        scratch_shapes=scratch,
        cost_estimate=less,
        compiler_params=pltpu.CompilerParams(vmem_limit_bytes=20 * MIB),
        name="far",
    )(*all_passages, mine_far, picks)
    cand_scores, send = pl.pallas_call(
        last_kernel,
        out_shape=(
            jax.ShapeDtypeStruct((slots, rows), jnp.float32),
            jax.ShapeDtypeStruct((2, slots // 2, rows), jnp.float32),
        ),
        in_specs=vmem(10),
        out_specs=tuple(vmem(2)),
        scratch_shapes=scratch + [pltpu.VMEM((rows // 2, doc_count), jnp.float32)],
        cost_estimate=less,
        compiler_params=pltpu.CompilerParams(vmem_limit_bytes=20 * MIB),
        name="last",
    )(*all_passages, theirs_far, picks, near, far, live)
    pieces = jnp.broadcast_to(send[None, :, None], (4, 2, 4) + send.shape[1:]).reshape(32, slots // 2, rows)
    pieces = lax.all_to_all(pieces, ("zh", "zl", "y"), 0, 0, tiled=True)
    falling, rising = pl.pallas_call(
        top_kernel,
        out_shape=(jax.ShapeDtypeStruct((128, rows), jnp.float32),) * 2,
        in_specs=vmem(1),
        out_specs=tuple(vmem(2)),
        compiler_params=pltpu.CompilerParams(vmem_limit_bytes=8 * MIB),
        name="top",
    )(pieces.reshape(-1, 8, rows))
    other = lax.ppermute(rising, "core", swap)
    merged = pl.pallas_call(
        merge_kernel,
        out_shape=jax.ShapeDtypeStruct((104, rows), jnp.float32),
        in_specs=vmem(2),
        out_specs=vmem(1)[0],
        compiler_params=pltpu.CompilerParams(vmem_limit_bytes=2 * MIB),
        name="merge",
    )(falling, other)
    top_scores = pl.pallas_call(
        join_kernel,
        out_shape=jax.ShapeDtypeStruct((TOPK, rows), jnp.float32),
        in_specs=vmem(2),
        out_specs=vmem(1)[0],
        compiler_params=pltpu.CompilerParams(vmem_limit_bytes=2 * MIB),
        name="join",
    )(merged, lax.ppermute(merged, "zl", swap))
    return (jnp.transpose(cand_scores), jnp.transpose(top_scores))


def solution(mesh):
    split = Mesh(mesh.devices.reshape(4, 2, 4, 2, 4), ALL)
    return jax.shard_map(
        shards,
        mesh=split,
        in_specs=(P("dim", SHARD),) * 4,
        out_specs=(P("dim", SHARD), P("dim", None)),
        check_vma=False,
    )
```
